256 devices in a mesh: pair: 64 (over z, y, core), rep: 4 (over x).
Axes of the slice: x: 4, y: 4, z: 8, core: 2. Of those that a mesh axis runs over, the one named last changes fastest.
Arguments:
- tau_ao: bfloat16 [4096, 65536], P('pair'), may hold values from -6 to 6
- slab_sizes: int32 [256], replicated, may hold values from 1 to 512, 65536 in all
- integrals: bfloat16 [256, 512, 1024], P('pair', 'rep'), may hold values from -0.0234375 to 0.0234375
- transform: float32 [1024, 512], replicated, may hold values from -0.1875 to 0.1875
Outputs:
- ladder_mo: float32 [4096, 512], P('pair', 'rep')
The draws below stay inside these ranges and needn't reach their ends.
Inputs may be any that keep to these rules, and one draw needn't show every extreme that they name: `slab_sizes`: the sizes sum to 65536 and the largest equals 512.
All inputs are finite; a program needn't handle non-finite values.
Results may differ from the reference program's by a relative error of at most 0.0003.
Values may be sent and summed in bfloat16 or wider, within the bound.
No kernel may reach another device: no remote copies, remote signals or barrier semaphores. Data moves between devices by JAX's collectives and lax.ppermute only.
A program may use at most 128 MiB of HBM per device.

```python
import math
import jax
import jax.numpy as jnp
import numpy as np
from jax import lax

SLAB_CAP = 512
NK = 1024
NV = 512
NPAIRS = 4096
NSLAB = 256
NQ = 65536


def block_levels(rng, extent, pieces, least, largest):
    factor_of = 1.0
    for axis_at, parts in pieces:
        steps = jax.random.uniform(jax.random.fold_in(jax.random.fold_in(rng, 6), axis_at), (parts,), jnp.float32, least / len(pieces), largest / len(pieces))
        factor_of = factor_of * jnp.repeat(jnp.exp(steps), extent[axis_at] // parts).reshape((-1,) + (1,) * (len(extent) - 1 - axis_at))
    return factor_of


def profile(amount, total, limit, lean):
    portions = [(1 << 20) // math.isqrt(grade ** lean) + 1 for grade in range(2, amount + 1)]
    rest, given = total - limit - (amount - 1), [1] * (amount - 1)
    while rest > 0:
        candidates = [i for i in range(amount - 1) if given[i] < limit]
        whole, left = sum([portions[i] for i in candidates]), rest
        for i in candidates:
            addition = min(limit - given[i], max(1, left * portions[i] // whole), rest)
            given[i] = given[i] + addition
            rest = rest - addition
    return np.array([limit] + given)


def ragged(rng, amount, total, reach, slope):
    if amount == 2:
        one = jax.random.randint(rng, (), max(1, total - reach), min(reach, total - 1) + 1)
        return jnp.stack([one, total - one])
    tallies = jnp.asarray(profile(amount, total, reach, slope), jnp.int32)
    twos = (amount - 1) // 2
    source_of, sink = tallies[1:1 + 2 * twos:2], tallies[2:2 + 2 * twos:2]
    slack = jnp.minimum(source_of - 1, reach - sink)
    shifted = jax.random.randint(jax.random.fold_in(rng, 1), (twos,), 0, 1 << 20) % (slack + 1)
    tallies = tallies.at[1:1 + 2 * twos:2].set(source_of - shifted).at[2:2 + 2 * twos:2].set(sink + shifted)
    return tallies[jax.random.permutation(jax.random.fold_in(rng, 2), amount)]


def normal_values(key, shape, scale, reach, split=(), kind=jnp.bfloat16):
    result = scale * jax.random.normal(key, shape, jnp.float32)
    if split:
        result = result * block_levels(key, shape, split, -0.22, 0.18)
    return jnp.clip(result, -reach, reach).astype(kind)


def setup_inputs(seed: int = 0) -> dict:
    splits = jax.random.split(jax.random.key(seed), 5)
    return {
        "tau_ao": normal_values(splits[0], (NPAIRS, NQ), 1.0, 6.0, ((0, 64),)),
        "slab_sizes": ragged(splits[1], NSLAB, NQ, SLAB_CAP, 2).astype(jnp.int32),
        "integrals": normal_values(splits[2], (NSLAB, SLAB_CAP, NK), NQ ** -0.5, 0.0234375, ((0, 64), (1, 4))),
        "transform": normal_values(splits[3], (NK, NV), NK ** -0.5, 0.1875, (), jnp.float32),
    }


def reference(tau_ao, slab_sizes, integrals, transform):
    sizes_int = slab_sizes.astype(jnp.int32)
    offsets = (jnp.cumsum(sizes_int) - sizes_int).astype(jnp.int32)
    slot_index = jnp.arange(SLAB_CAP, dtype=jnp.int32)

    def add_slab(ladder, entry):
        first_col, col_count, slab_block = entry
        columns = jnp.clip(first_col + slot_index, 0, NQ - 1).astype(jnp.int32)
        picked = jnp.take(tau_ao, columns, axis=1)
        picked = jnp.where(slot_index[None, :] < col_count, picked, jnp.zeros_like(picked))
        product = jnp.dot(picked.astype(jnp.float32), slab_block.astype(jnp.float32), precision=lax.Precision.HIGHEST)
        return ladder + product, None

    ladder, unused = lax.scan(add_slab, jnp.zeros((NPAIRS, NK), jnp.float32), (offsets, sizes_int, integrals))
    return jnp.dot(ladder, transform, precision=lax.Precision.HIGHEST)
```

```python
import functools

import jax
import jax.numpy as jnp
from jax import lax
from jax.experimental import pallas as pl
from jax.experimental.pallas import tpu as pltpu
from jax.sharding import Mesh
from jax.sharding import PartitionSpec as P

LANES = 128
PAD = 16
VMEM = 56 * 1024 * 1024
SHIFTS = (64, 32, 16, 8, 4, 2, 1)
TOP = 8.0
FRACTION = 12


def power(exponent, sign):
    out = jnp.ones_like(exponent)
    for bit in SHIFTS:
        has = exponent >= bit
        out = jnp.where(has, out * (2.0 ** (sign * bit)), out)
        exponent = jnp.where(has, exponent - bit, exponent)
    return out


def split3(value):
    first = value.astype(jnp.bfloat16)
    rest = value - first.astype(jnp.float32)
    second = rest.astype(jnp.bfloat16)
    third = (rest - second.astype(jnp.float32)).astype(jnp.bfloat16)
    return first, second, third


def fold_kernel(slab_ref, transform_ref, out_ref):
    rows = slab_ref[...]
    terms = split3(transform_ref[...])
    folded = sum(jnp.dot(rows, t, preferred_element_type=jnp.float32) for t in reversed(terms))
    peak = jnp.max(jnp.abs(folded), axis=1, keepdims=True)
    exponent = jnp.zeros_like(peak)
    for bit in SHIFTS:
        fits = (peak * (2.0 ** bit) < TOP) & (exponent + bit <= 96)
        peak = jnp.where(fits, peak * (2.0 ** bit), peak)
        exponent = jnp.where(fits, exponent + bit, exponent)
    scaled = folded * power(exponent, 1) * (2.0 ** FRACTION)
    codes = jnp.clip(jnp.round(scaled), -32767.0, 32767.0)
    count = rows.shape[0]
    out_ref[:count] = codes.astype(jnp.int32).astype(jnp.int16)
    across = jnp.transpose(jnp.broadcast_to(exponent, (count, LANES)))
    out_ref[count:] = across[:PAD].astype(jnp.int32).astype(jnp.int16)


def fold(slabs, transform):
    rows, cols = slabs.shape[0], transform.shape[1]
    return pl.pallas_call(
        fold_kernel,
        out_shape=jax.ShapeDtypeStruct((rows + PAD, cols), jnp.int16),
        compiler_params=pltpu.CompilerParams(vmem_limit_bytes=VMEM),
        cost_estimate=pl.CostEstimate(flops=6 * rows * slabs.shape[1] * cols, bytes_accessed=4 << 20, transcendentals=0),
        name="fold",
    )(slabs, transform)


def pick_kernel(per_device, width, sizes_ref, rep_ref, tau_ref, out_ref, offset_ref):
    group, groups = pl.program_id(0), pl.num_programs(0)
    slabs = sizes_ref.shape[0]

    @pl.when(group == 0)
    def _():
        def step(s, total):
            offset_ref[s] = total
            return total + sizes_ref[s]

        lax.fori_loop(0, slabs, step, jnp.int32(0))

    start = rep_ref[0] * width
    last = tau_ref.shape[1] // LANES - 2
    lane = lax.broadcasted_iota(jnp.int32, (tau_ref.shape[0], LANES), 1)

    def one(n, carry):
        slab = (n // per_device * groups + group) * per_device + n % per_device
        base = offset_ref[slab] + start
        block = jnp.minimum(base // LANES, last)
        shift = jnp.minimum(base - block * LANES, 2 * LANES - 1)
        window = tau_ref[:, pl.ds(pl.multiple_of(block * LANES, LANES), 2 * LANES)].astype(jnp.float32)
        moved = pltpu.roll(window, 2 * LANES - shift, axis=1)[:, :LANES]
        kept = jnp.where(lane < sizes_ref[slab] - start, moved, 0.0)
        out_ref[0, :, pl.ds(pl.multiple_of(n * LANES, LANES), LANES)] = kept.astype(jnp.bfloat16)
        return carry

    lax.fori_loop(0, slabs // groups, one, 0)


def pick(tau, sizes, rep, groups, per_device, width):
    rows, cols = tau.shape[0], sizes.shape[0] // groups * width
    return pl.pallas_call(
        functools.partial(pick_kernel, per_device, width),
        grid_spec=pltpu.PrefetchScalarGridSpec(
            num_scalar_prefetch=2,
            grid=(groups,),
            in_specs=[pl.BlockSpec(tau.shape, lambda g, *_: (0, 0), pipeline_mode=pl.Buffered(1))],
            out_specs=pl.BlockSpec((1, rows, cols), lambda g, *_: (g, 0, 0)),
            scratch_shapes=[pltpu.SMEM((sizes.shape[0],), jnp.int32)],
        ),
        out_shape=jax.ShapeDtypeStruct((groups, rows, cols), jnp.bfloat16),
        compiler_params=pltpu.CompilerParams(vmem_limit_bytes=VMEM),
        cost_estimate=pl.CostEstimate(flops=0, bytes_accessed=12 << 20, transcendentals=0),
        name="pick",
    )(sizes, rep, tau)


def contract_kernel(amps_ref, coded_ref, out_ref):
    depth = amps_ref.shape[1]
    reps = out_ref.shape[1]

    @pl.when(pl.program_id(0) == 0)
    def _():
        out_ref[...] = jnp.zeros_like(out_ref)

    code = coded_ref[0, :depth].astype(jnp.int32).astype(jnp.float32)
    high = code.astype(jnp.bfloat16)
    low = (code - high.astype(jnp.float32)).astype(jnp.bfloat16)
    exponent = coded_ref[0, depth:].astype(jnp.int32).astype(jnp.float32)[:1]
    scale = power(exponent, -1) * (2.0 ** -FRACTION)
    amps = (amps_ref[...].astype(jnp.float32) * scale).astype(jnp.bfloat16)
    part = jnp.dot(amps, high, preferred_element_type=jnp.float32)
    part = part + jnp.dot(amps, low, preferred_element_type=jnp.float32)
    rows = out_ref.shape[2]
    for g in range(out_ref.shape[0]):
        for r in range(reps):
            out_ref[g, r] += part[g * rows:(g + 1) * rows, r * LANES:(r + 1) * LANES]


def contract(amps, coded, groups, reps):
    chunks, padded, cols = coded.shape
    depth = padded - PAD
    shape = (groups, reps, amps.shape[0] // groups, cols // reps)
    return pl.pallas_call(
        contract_kernel,
        grid=(chunks,),
        in_specs=[
            pl.BlockSpec((amps.shape[0], depth), lambda k: (0, k)),
            pl.BlockSpec((1, padded, cols), lambda k: (k, 0, 0)),
        ],
        out_specs=pl.BlockSpec(shape, lambda k: (0, 0, 0, 0)),
        out_shape=jax.ShapeDtypeStruct(shape, jnp.float32),
        compiler_params=pltpu.CompilerParams(vmem_limit_bytes=VMEM),
        cost_estimate=pl.CostEstimate(flops=4 * amps.size * cols, bytes_accessed=9 << 20, transcendentals=0),
        name="contract",
    )(amps, coded)


def body(tau_ao, slab_sizes, integrals, transform):
    groups = lax.axis_size("y") * lax.axis_size("core")
    reps = lax.axis_size("rep")
    per_device, width, depth = integrals.shape
    coded = fold(integrals.reshape(per_device * width, depth), transform)
    line = lax.all_gather(coded, "z", axis=0, tiled=False)
    rep = lax.axis_index("rep").reshape(1)
    picked = pick(tau_ao, slab_sizes, rep, groups, per_device, width)
    arrived = lax.all_to_all(picked, ("y", "core"), split_axis=0, concat_axis=0, tiled=True)
    amps = arrived.reshape(-1, arrived.shape[-1])
    partial = contract(amps, line, groups, reps)
    partial = partial.reshape(groups * reps, *partial.shape[2:])
    shares = lax.all_to_all(partial, ("y", "core", "rep"), split_axis=0, concat_axis=0, tiled=True)
    return jnp.sum(shares, axis=0)


def solution(mesh):
    fine = Mesh(mesh.devices.reshape(8, 4, 2, 4), ("z", "y", "core", "rep"))
    pair = ("z", "y", "core")
    return jax.shard_map(
        body,
        mesh=fine,
        in_specs=(P(pair, None), P(), P(pair, "rep", None), P()),
        out_specs=P(pair, "rep"),
        check_vma=False,
    )
```

```python
import functools

import jax
import jax.numpy as jnp
from jax import lax
from jax.experimental import pallas as pl
from jax.experimental.pallas import tpu as pltpu
from jax.sharding import Mesh
from jax.sharding import PartitionSpec as P

LANES = 128
PAD = 16
VMEM = 56 * 1024 * 1024
SHIFTS = (64, 32, 16, 8, 4, 2, 1)
TOP = 8.0
FRACTION = 12


def power(exponent, sign):
    out = jnp.ones_like(exponent)
    for bit in SHIFTS:
        has = exponent >= bit
        out = jnp.where(has, out * (2.0 ** (sign * bit)), out)
        exponent = jnp.where(has, exponent - bit, exponent)
    return out


def split2(value):
    first = value.astype(jnp.bfloat16)
    return first, (value - first.astype(jnp.float32)).astype(jnp.bfloat16)


def fold_kernel(slab_ref, transform_ref, out_ref):
    rows = slab_ref[...]
    high, low = split2(transform_ref[...])
    folded = jnp.dot(rows, low, preferred_element_type=jnp.float32)
    folded = folded + jnp.dot(rows, high, preferred_element_type=jnp.float32)
    peak = jnp.max(jnp.abs(folded), axis=1, keepdims=True)
    exponent = jnp.zeros_like(peak)
    for bit in SHIFTS:
        fits = (peak * (2.0 ** bit) < TOP) & (exponent + bit <= 96)
        peak = jnp.where(fits, peak * (2.0 ** bit), peak)
        exponent = jnp.where(fits, exponent + bit, exponent)
    scaled = folded * power(exponent, 1) * (2.0 ** FRACTION)
    codes = jnp.clip(jnp.round(scaled), -32767.0, 32767.0)
    count = rows.shape[0]
    out_ref[:count] = codes.astype(jnp.int32).astype(jnp.int16)
    across = jnp.transpose(jnp.broadcast_to(exponent, (count, LANES)))
    out_ref[count:] = across[:PAD].astype(jnp.int32).astype(jnp.int16)


def fold(slabs, transform):
    rows, cols = slabs.shape[0], transform.shape[1]
    return pl.pallas_call(
        fold_kernel,
        out_shape=jax.ShapeDtypeStruct((rows + PAD, cols), jnp.int16),
        compiler_params=pltpu.CompilerParams(vmem_limit_bytes=VMEM),
        cost_estimate=pl.CostEstimate(flops=4 * rows * slabs.shape[1] * cols, bytes_accessed=4 << 20, transcendentals=0),
        name="fold",
    )(slabs, transform)


def pick_kernel(per_device, width, sizes_ref, rep_ref, tau_hbm, out_hbm, low_ref, turn_ref, left_ref, tau_ref, stage_ref, tau_sem, out_sem):
    slabs, packed, groups = sizes_ref.shape[0], tau_ref.shape[1], stage_ref.shape[0]
    load = pltpu.make_async_copy(tau_hbm, tau_ref, tau_sem)
    load.start()
    start = rep_ref[0] * width

    def place(s, base):
        low = jnp.minimum((base + start) & -LANES, packed - 2 * LANES)
        low_ref[s] = low
        turn_ref[s] = 2 * LANES - jnp.minimum(base + start - low, 2 * LANES - 1)
        size = sizes_ref[s]
        left_ref[s] = size - start
        return base + size

    lax.fori_loop(0, slabs, place, jnp.int32(0), unroll=16)
    load.wait()
    lane = lax.broadcasted_iota(jnp.int32, (tau_ref.shape[0], LANES), 1)
    stores = []
    for group in range(groups):
        for n in range(slabs // groups):
            slab = (n // per_device * groups + group) * per_device + n % per_device
            window = tau_ref[:, pl.ds(pl.multiple_of(low_ref[slab], LANES), 2 * LANES)]
            moved = pltpu.roll(window, turn_ref[slab], axis=1)[:, :LANES]
            stage_ref[group, :, n * LANES:(n + 1) * LANES] = jnp.where(lane < left_ref[slab], moved, jnp.zeros_like(moved))
        store = pltpu.make_async_copy(stage_ref.at[group], out_hbm.at[group], out_sem.at[group])
        store.start()
        stores.append(store)
    for store in stores:
        store.wait()


def pick(tau, sizes, rep, groups, per_device, width):
    slabs = sizes.shape[0]
    shape = (groups, tau.shape[0], slabs // groups * width)
    return pl.pallas_call(
        functools.partial(pick_kernel, per_device, width),
        in_specs=[pl.BlockSpec(memory_space=pltpu.SMEM)] * 2 + [pl.BlockSpec(memory_space=pl.ANY)],
        out_specs=pl.BlockSpec(memory_space=pl.ANY),
        out_shape=jax.ShapeDtypeStruct(shape, jnp.bfloat16),
        scratch_shapes=[pltpu.SMEM((slabs,), jnp.int32)] * 3
        + [
            pltpu.VMEM(tau.shape, jnp.bfloat16),
            pltpu.VMEM(shape, jnp.bfloat16),
            pltpu.SemaphoreType.DMA,
            pltpu.SemaphoreType.DMA((groups,)),
        ],
        compiler_params=pltpu.CompilerParams(vmem_limit_bytes=VMEM),
        cost_estimate=pl.CostEstimate(flops=0, bytes_accessed=12 << 20, transcendentals=0),
        name="pick",
    )(sizes, rep, tau)


def contract_kernel(amps_ref, coded_ref, out_ref):
    chunks, depth = coded_ref.shape[0], coded_ref.shape[1] - PAD

    @pl.when(pl.program_id(0) == 0)
    def _():
        out_ref[...] = jnp.zeros_like(out_ref)

    part = None
    for n in range(chunks):
        code = coded_ref[n, :depth].astype(jnp.int32).astype(jnp.float32)
        exponent = coded_ref[n, depth:].astype(jnp.int32).astype(jnp.float32)[:1]
        scale = power(exponent, -1) * (2.0 ** -FRACTION)
        amps = (amps_ref[:, n * depth:(n + 1) * depth].astype(jnp.float32) * scale).astype(jnp.bfloat16)
        for term in split2(code):
            more = jnp.dot(amps, term, preferred_element_type=jnp.float32)
            part = more if part is None else part + more
    groups, reps, rows, cols = out_ref.shape
    for g in range(groups):
        for r in range(reps):
            out_ref[g, r] += part[g * rows:(g + 1) * rows, r * cols:(r + 1) * cols]


def contract(amps, coded, groups, reps):
    chunks, padded, cols = coded.shape
    depth = padded - PAD
    step = 2
    shape = (groups, reps, amps.shape[0] // groups, cols // reps)
    return pl.pallas_call(
        contract_kernel,
        grid=(chunks // step,),
        in_specs=[
            pl.BlockSpec((amps.shape[0], step * depth), lambda k: (0, k)),
            pl.BlockSpec((step, padded, cols), lambda k: (k, 0, 0)),
        ],
        out_specs=pl.BlockSpec(shape, lambda k: (0, 0, 0, 0)),
        out_shape=jax.ShapeDtypeStruct(shape, jnp.float32),
        compiler_params=pltpu.CompilerParams(vmem_limit_bytes=VMEM),
        cost_estimate=pl.CostEstimate(flops=4 * amps.size * cols, bytes_accessed=9 << 20, transcendentals=0),
        name="contract",
    )(amps, coded)


def body(tau_ao, slab_sizes, integrals, transform):
    groups = lax.axis_size("y") * lax.axis_size("core")
    reps = lax.axis_size("rep")
    per_device, width, depth = integrals.shape
    coded = fold(integrals.reshape(per_device * width, depth), transform)
    line = lax.all_gather(coded, "z", axis=0, tiled=False)
    rep = lax.axis_index("rep").reshape(1)
    picked = pick(tau_ao, slab_sizes, rep, groups, per_device, width)
    arrived = lax.all_to_all(picked, ("y", "core"), split_axis=0, concat_axis=0, tiled=True)
    amps = arrived.reshape(-1, arrived.shape[-1])
    partial = contract(amps, line, groups, reps)
    partial = partial.reshape(groups * reps, *partial.shape[2:])
    shares = lax.all_to_all(partial, ("y", "core", "rep"), split_axis=0, concat_axis=0, tiled=True)
    return jnp.sum(shares, axis=0)


def solution(mesh):
    fine = Mesh(mesh.devices.reshape(8, 4, 2, 4), ("z", "y", "core", "rep"))
    pair = ("z", "y", "core")
    return jax.shard_map(
        body,
        mesh=fine,
        in_specs=(P(pair, None), P(), P(pair, "rep", None), P()),
        out_specs=P(pair, "rep"),
        check_vma=False,
    )
```

```python
import functools

import jax
import jax.numpy as jnp
from jax import lax
from jax.experimental import pallas as pl
from jax.experimental.pallas import tpu as pltpu
from jax.sharding import Mesh
from jax.sharding import PartitionSpec as P

LANES = 128
PAD = 16
VMEM = 56 * 1024 * 1024
SHIFTS = (64, 32, 16, 8, 4, 2, 1)
TOP = 8.0
FRACTION = 12


def power(exponent, sign):
    out = jnp.ones_like(exponent)
    for bit in SHIFTS:
        has = exponent >= bit
        out = jnp.where(has, out * (2.0 ** (sign * bit)), out)
        exponent = jnp.where(has, exponent - bit, exponent)
    return out


def split2(value):
    first = value.astype(jnp.bfloat16)
    return first, (value - first.astype(jnp.float32)).astype(jnp.bfloat16)


def fold_kernel(slab_ref, transform_ref, out_ref):
    rows = slab_ref[...]
    high, low = split2(transform_ref[...])
    folded = jnp.dot(rows, low, preferred_element_type=jnp.float32)
    folded = folded + jnp.dot(rows, high, preferred_element_type=jnp.float32)
    peak = jnp.max(jnp.abs(folded), axis=1, keepdims=True)
    exponent = jnp.zeros_like(peak)
    for bit in SHIFTS:
        fits = (peak * (2.0 ** bit) < TOP) & (exponent + bit <= 96)
        peak = jnp.where(fits, peak * (2.0 ** bit), peak)
        exponent = jnp.where(fits, exponent + bit, exponent)
    scaled = folded * power(exponent, 1) * (2.0 ** FRACTION)
    codes = jnp.clip(jnp.round(scaled), -32767.0, 32767.0)
    count = rows.shape[0]
    out_ref[:count] = codes.astype(jnp.int32).astype(jnp.int16)
    across = jnp.transpose(jnp.broadcast_to(exponent, (count, LANES)))
    out_ref[count:] = across[:PAD].astype(jnp.int32).astype(jnp.int16)


def fold(slabs, transform):
    rows, cols = slabs.shape[0], transform.shape[1]
    return pl.pallas_call(
        fold_kernel,
        out_shape=jax.ShapeDtypeStruct((rows + PAD, cols), jnp.int16),
        compiler_params=pltpu.CompilerParams(vmem_limit_bytes=16 << 20),
        cost_estimate=pl.CostEstimate(flops=4 * rows * slabs.shape[1] * cols, bytes_accessed=4 << 20, transcendentals=0),
        name="fold",
    )(slabs, transform)


def pick_kernel(per_device, width, sizes_ref, rep_ref, tau_hbm, out_hbm, low_ref, turn_ref, left_ref, tau_ref, stage_ref, tau_sems, out_sems):
    slabs, packed, groups = sizes_ref.shape[0], tau_ref.shape[1], stage_ref.shape[0]
    pieces, lines = tau_sems.shape[0], out_sems.shape[0]
    piece, span = packed // pieces, per_device * width

    def load(k):
        columns = pl.ds(pl.multiple_of(k * piece, piece), piece)
        return pltpu.make_async_copy(tau_hbm.at[:, columns], tau_ref.at[:, columns], tau_sems.at[k])

    for k in range(pieces):
        load(k).start()
    start = rep_ref[0] * width

    def place(s, base):
        low = jnp.minimum((base + start) & -LANES, packed - 2 * LANES)
        low_ref[s] = low
        turn_ref[s] = 2 * LANES - jnp.minimum(base + start - low, 2 * LANES - 1)
        size = sizes_ref[s]
        left_ref[s] = size - start
        return base + size

    lax.fori_loop(0, slabs, place, jnp.int32(0), unroll=16)
    lane = lax.broadcasted_iota(jnp.int32, (tau_ref.shape[0], LANES), 1)

    def arrive(k, carry):
        load(k).wait()
        return carry

    stores, have = [], jnp.int32(0)
    for z in range(lines):
        end = low_ref[(z + 1) * groups * per_device - 1] + 2 * LANES
        need = lax.div(end + piece - 1, piece) if z < lines - 1 else jnp.int32(pieces)
        lax.fori_loop(have, need, arrive, 0)
        have = need
        for group in range(groups):
            for i in range(per_device):
                slab = (z * groups + group) * per_device + i
                column = z * span + i * width
                window = tau_ref[:, pl.ds(pl.multiple_of(low_ref[slab], LANES), 2 * LANES)]
                moved = pltpu.roll(window, turn_ref[slab], axis=1)[:, :LANES]
                stage_ref[group, :, column:column + LANES] = jnp.where(lane < left_ref[slab], moved, jnp.zeros_like(moved))
        columns = pl.ds(z * span, span)
        store = pltpu.make_async_copy(stage_ref.at[:, :, columns], out_hbm.at[:, :, columns], out_sems.at[z])
        store.start()
        stores.append(store)
    for store in stores:
        store.wait()


def pick(tau, sizes, rep, groups, per_device, width):
    slabs = sizes.shape[0]
    lines = slabs // groups // per_device
    shape = (groups, tau.shape[0], lines * per_device * width)
    return pl.pallas_call(
        functools.partial(pick_kernel, per_device, width),
        in_specs=[pl.BlockSpec(memory_space=pltpu.SMEM)] * 2 + [pl.BlockSpec(memory_space=pl.ANY)],
        out_specs=pl.BlockSpec(memory_space=pl.ANY),
        out_shape=jax.ShapeDtypeStruct(shape, jnp.bfloat16),
        scratch_shapes=[pltpu.SMEM((slabs,), jnp.int32)] * 3
        + [
            pltpu.VMEM(tau.shape, jnp.bfloat16),
            pltpu.VMEM(shape, jnp.bfloat16),
            pltpu.SemaphoreType.DMA((8,)),
            pltpu.SemaphoreType.DMA((lines,)),
        ],
        compiler_params=pltpu.CompilerParams(vmem_limit_bytes=VMEM),
        cost_estimate=pl.CostEstimate(flops=0, bytes_accessed=12 << 20, transcendentals=0),
        name="pick",
    )(sizes, rep, tau)


def contract_kernel(step, core_ref, amps_hbm, coded_hbm, out_ref, amps_ref, coded_ref, amps_sems, coded_sems):
    chunks, depth = coded_ref.shape[0], coded_ref.shape[1] - PAD
    ys, reps, rows, cols = out_ref.shape
    stride = amps_hbm.shape[0] // ys
    loads = []
    for n in range(chunks // step):
        columns = pl.ds(n * step * depth, step * depth)
        load = [pltpu.make_async_copy(coded_hbm.at[pl.ds(n * step, step)], coded_ref.at[pl.ds(n * step, step)], coded_sems.at[n])]
        for y in range(ys):
            source = amps_hbm.at[y * stride + core_ref[0], :, columns]
            load.append(pltpu.make_async_copy(source, amps_ref.at[y, :, columns], amps_sems.at[n, y]))
        loads.append(load)
    for load in loads:
        for copy in load:
            copy.start()
    total = None
    for n, load in enumerate(loads):
        for copy in load:
            copy.wait()
        for k in range(n * step, (n + 1) * step):
            code = coded_ref[k, :depth].astype(jnp.int32).astype(jnp.float32)
            exponent = coded_ref[k, depth:].astype(jnp.int32).astype(jnp.float32)[:1]
            scale = power(exponent, -1) * (2.0 ** -FRACTION)
            amps = amps_ref[:, :, k * depth:(k + 1) * depth].reshape(ys * rows, depth)
            amps = (amps.astype(jnp.float32) * scale).astype(jnp.bfloat16)
            for term in split2(code):
                more = jnp.dot(amps, term, preferred_element_type=jnp.float32)
                total = more if total is None else total + more
    for y in range(ys):
        for r in range(reps):
            out_ref[y, r] = total[y * rows:(y + 1) * rows, r * cols:(r + 1) * cols]


def contract(amps, coded, core, ys, reps, grant):
    chunks, padded, cols = coded.shape
    groups, rows, depth = amps.shape
    step = 2
    shape = (ys, reps, rows, cols // reps)
    return pl.pallas_call(
        functools.partial(contract_kernel, step),
        in_specs=[pl.BlockSpec(memory_space=pltpu.SMEM)] + [pl.BlockSpec(memory_space=pl.ANY)] * 2,
        out_specs=pl.BlockSpec(memory_space=pltpu.VMEM),
        out_shape=jax.ShapeDtypeStruct(shape, jnp.float32),
        scratch_shapes=[
            pltpu.VMEM((ys, rows, depth), jnp.bfloat16),
            pltpu.VMEM(coded.shape, jnp.int16),
            pltpu.SemaphoreType.DMA((chunks // step, ys)),
            pltpu.SemaphoreType.DMA((chunks // step,)),
        ],
        compiler_params=pltpu.CompilerParams(vmem_limit_bytes=grant << 20),
        cost_estimate=pl.CostEstimate(flops=4 * ys * rows * depth * cols, bytes_accessed=7 << 20, transcendentals=0),
        name="contract",
    )(core.reshape(1), amps, coded)


def body(tau_ao, slab_sizes, integrals, transform):
    groups = lax.axis_size("y") * lax.axis_size("core")
    reps = lax.axis_size("rep")
    per_device, width, depth = integrals.shape
    coded = fold(integrals.reshape(per_device * width, depth), transform)
    line = lax.all_gather(coded, "z", axis=0, tiled=False)
    rep = lax.axis_index("rep").reshape(1)
    picked = pick(tau_ao, slab_sizes, rep, groups, per_device, width)
    arrived = lax.all_to_all(picked, ("y", "core"), split_axis=0, concat_axis=0, tiled=True)
    core, ys = lax.axis_index("core"), lax.axis_size("y")
    theirs = contract(arrived, line, 1 - core, ys, reps, 50)
    theirs = lax.ppermute(theirs, "core", [(0, 1), (1, 0)])
    partial = contract(arrived, line, core, ys, reps, 32) + theirs
    partial = partial.reshape(ys * reps, *partial.shape[2:])
    shares = lax.all_to_all(partial, ("y", "rep"), split_axis=0, concat_axis=0, tiled=True)
    return jnp.sum(shares, axis=0)


def solution(mesh):
    fine = Mesh(mesh.devices.reshape(8, 4, 2, 4), ("z", "y", "core", "rep"))
    pair = ("z", "y", "core")
    return jax.shard_map(
        body,
        mesh=fine,
        in_specs=(P(pair, None), P(), P(pair, "rep", None), P()),
        out_specs=P(pair, "rep"),
        check_vma=False,
    )
```

```python
import functools

import jax
import jax.numpy as jnp
from jax import lax
from jax.experimental import pallas as pl
from jax.experimental.pallas import tpu as pltpu
from jax.sharding import Mesh
from jax.sharding import PartitionSpec as P

LANES = 128
PAD = 16
VMEM = 56 * 1024 * 1024
SHIFTS = (64, 32, 16, 8, 4, 2, 1)
TOP = 8.0
FRACTION = 12


def power(exponent, sign):
    out = jnp.ones_like(exponent)
    for bit in SHIFTS:
        has = exponent >= bit
        out = jnp.where(has, out * (2.0 ** (sign * bit)), out)
        exponent = jnp.where(has, exponent - bit, exponent)
    return out


def split2(value):
    first = value.astype(jnp.bfloat16)
    return first, (value - first.astype(jnp.float32)).astype(jnp.bfloat16)


def fold_kernel(slab_ref, transform_ref, out_ref):
    rows = slab_ref[...]
    high, low = split2(transform_ref[...])
    folded = jnp.dot(rows, low, preferred_element_type=jnp.float32)
    folded = folded + jnp.dot(rows, high, preferred_element_type=jnp.float32)
    peak = jnp.max(jnp.abs(folded), axis=1, keepdims=True)
    exponent = jnp.zeros_like(peak)
    for bit in SHIFTS:
        fits = (peak * (2.0 ** bit) < TOP) & (exponent + bit <= 96)
        peak = jnp.where(fits, peak * (2.0 ** bit), peak)
        exponent = jnp.where(fits, exponent + bit, exponent)
    scaled = folded * power(exponent, 1) * (2.0 ** FRACTION)
    codes = jnp.clip(jnp.round(scaled), -32767.0, 32767.0)
    count = rows.shape[0]
    out_ref[:count] = codes.astype(jnp.int32).astype(jnp.int16)
    across = jnp.transpose(jnp.broadcast_to(exponent, (count, LANES)))
    out_ref[count:] = across[:PAD].astype(jnp.int32).astype(jnp.int16)


def fold(slabs, transform):
    rows, cols = slabs.shape[0], transform.shape[1]
    return pl.pallas_call(
        fold_kernel,
        out_shape=jax.ShapeDtypeStruct((rows + PAD, cols), jnp.int16),
        compiler_params=pltpu.CompilerParams(vmem_limit_bytes=16 << 20),
        cost_estimate=pl.CostEstimate(flops=4 * rows * slabs.shape[1] * cols, bytes_accessed=4 << 20, transcendentals=0),
        name="fold",
    )(slabs, transform)


def pick_kernel(per_device, width, sizes_ref, rep_ref, tau_hbm, out_hbm, low_ref, turn_ref, left_ref, tau_ref, stage_ref, tau_sems, out_sems):
    slabs, packed, groups = sizes_ref.shape[0], tau_ref.shape[1], stage_ref.shape[0]
    pieces, lines = tau_sems.shape[0], out_sems.shape[0]
    piece, span = packed // pieces, per_device * width

    def load(k):
        columns = pl.ds(pl.multiple_of(k * piece, piece), piece)
        return pltpu.make_async_copy(tau_hbm.at[:, columns], tau_ref.at[:, columns], tau_sems.at[k])

    for k in range(pieces):
        load(k).start()
    start = rep_ref[0] * width

    def place(s, base):
        low = jnp.minimum((base + start) & -LANES, packed - 2 * LANES)
        low_ref[s] = low
        turn_ref[s] = 2 * LANES - jnp.minimum(base + start - low, 2 * LANES - 1)
        size = sizes_ref[s]
        left_ref[s] = size - start
        return base + size

    lax.fori_loop(0, slabs, place, jnp.int32(0), unroll=16)
    lane = lax.broadcasted_iota(jnp.int32, (tau_ref.shape[0], LANES), 1)

    def arrive(k, carry):
        load(k).wait()
        return carry

    stores, have = [], jnp.int32(0)
    for z in range(lines):
        end = low_ref[(z + 1) * groups * per_device - 1] + 2 * LANES
        need = lax.div(end + piece - 1, piece) if z < lines - 1 else jnp.int32(pieces)
        lax.fori_loop(have, need, arrive, 0)
        have = need
        for group in range(groups):
            for i in range(per_device):
                slab = (z * groups + group) * per_device + i
                column = z * span + i * width
                window = tau_ref[:, pl.ds(pl.multiple_of(low_ref[slab], LANES), 2 * LANES)]
                moved = pltpu.roll(window, turn_ref[slab], axis=1)[:, :LANES]
                stage_ref[group, :, column:column + LANES] = jnp.where(lane < left_ref[slab], moved, jnp.zeros_like(moved))
        columns = pl.ds(z * span, span)
        store = pltpu.make_async_copy(stage_ref.at[:, :, columns], out_hbm.at[:, :, columns], out_sems.at[z])
        store.start()
        stores.append(store)
    for store in stores:
        store.wait()


def pick(tau, sizes, rep, groups, per_device, width):
    slabs = sizes.shape[0]
    lines = slabs // groups // per_device
    shape = (groups, tau.shape[0], lines * per_device * width)
    return pl.pallas_call(
        functools.partial(pick_kernel, per_device, width),
        in_specs=[pl.BlockSpec(memory_space=pltpu.SMEM)] * 2 + [pl.BlockSpec(memory_space=pl.ANY)],
        out_specs=pl.BlockSpec(memory_space=pl.ANY),
        out_shape=jax.ShapeDtypeStruct(shape, jnp.bfloat16),
        scratch_shapes=[pltpu.SMEM((slabs,), jnp.int32)] * 3
        + [
            pltpu.VMEM(tau.shape, jnp.bfloat16),
            pltpu.VMEM(shape, jnp.bfloat16),
            pltpu.SemaphoreType.DMA((8,)),
            pltpu.SemaphoreType.DMA((lines,)),
        ],
        compiler_params=pltpu.CompilerParams(vmem_limit_bytes=VMEM),
        cost_estimate=pl.CostEstimate(flops=0, bytes_accessed=12 << 20, transcendentals=0),
        name="pick",
    )(sizes, rep, tau)


def contract_kernel(step, core_ref, amps_hbm, coded_hbm, out_ref, amps_ref, coded_ref, amps_sems, coded_sems):
    chunks, depth = coded_ref.shape[0], coded_ref.shape[1] - PAD
    ys, reps, rows, cols = out_ref.shape
    stride = amps_hbm.shape[0] // ys
    loads = []
    for n in range(chunks // step):
        columns = pl.ds(n * step * depth, step * depth)
        load = [pltpu.make_async_copy(coded_hbm.at[pl.ds(n * step, step)], coded_ref.at[pl.ds(n * step, step)], coded_sems.at[n])]
        for y in range(ys):
            source = amps_hbm.at[y * stride + core_ref[0], :, columns]
            load.append(pltpu.make_async_copy(source, amps_ref.at[y, :, columns], amps_sems.at[n, y]))
        loads.append(load)
    for load in loads:
        for copy in load:
            copy.start()
    total = None
    for n, load in enumerate(loads):
        for copy in load:
            copy.wait()
        for k in range(n * step, (n + 1) * step):
            code = coded_ref[k, :depth].astype(jnp.int32).astype(jnp.float32)
            exponent = coded_ref[k, depth:].astype(jnp.int32).astype(jnp.float32)[:1]
            scale = power(exponent, -1) * (2.0 ** -FRACTION)
            amps = amps_ref[:, :, k * depth:(k + 1) * depth].reshape(ys * rows, depth)
            amps = amps * scale.astype(jnp.bfloat16)
            for term in split2(code):
                more = jnp.dot(amps, term, preferred_element_type=jnp.float32)
                total = more if total is None else total + more
    for y in range(ys):
        for r in range(reps):
            out_ref[y, r] = total[y * rows:(y + 1) * rows, r * cols:(r + 1) * cols]


def contract(amps, coded, core, ys, reps, grant):
    chunks, padded, cols = coded.shape
    groups, rows, depth = amps.shape
    step = 2
    shape = (ys, reps, rows, cols // reps)
    return pl.pallas_call(
        functools.partial(contract_kernel, step),
        in_specs=[pl.BlockSpec(memory_space=pltpu.SMEM)] + [pl.BlockSpec(memory_space=pl.ANY)] * 2,
        out_specs=pl.BlockSpec(memory_space=pltpu.VMEM),
        out_shape=jax.ShapeDtypeStruct(shape, jnp.float32),
        scratch_shapes=[
            pltpu.VMEM((ys, rows, depth), jnp.bfloat16),
            pltpu.VMEM(coded.shape, jnp.int16),
            pltpu.SemaphoreType.DMA((chunks // step, ys)),
            pltpu.SemaphoreType.DMA((chunks // step,)),
        ],
        compiler_params=pltpu.CompilerParams(vmem_limit_bytes=grant << 20),
        cost_estimate=pl.CostEstimate(flops=4 * ys * rows * depth * cols, bytes_accessed=7 << 20, transcendentals=0),
        name="contract",
    )(core.reshape(1), amps, coded)


def body(tau_ao, slab_sizes, integrals, transform):
    groups = lax.axis_size("y") * lax.axis_size("core")
    reps = lax.axis_size("rep")
    per_device, width, depth = integrals.shape
    coded = fold(integrals.reshape(per_device * width, depth), transform)
    line = lax.all_gather(coded, "z", axis=0, tiled=False)
    rep = lax.axis_index("rep").reshape(1)
    picked = pick(tau_ao, slab_sizes, rep, groups, per_device, width)
    arrived = lax.all_to_all(picked, ("y", "core"), split_axis=0, concat_axis=0, tiled=True)
    core, ys = lax.axis_index("core"), lax.axis_size("y")
    theirs = contract(arrived, line, 1 - core, ys, reps, 50)
    theirs = lax.ppermute(theirs, "core", [(0, 1), (1, 0)])
    partial = contract(arrived, line, core, ys, reps, 32) + theirs
    partial = partial.reshape(ys * reps, *partial.shape[2:])
    shares = lax.all_to_all(partial, ("y", "rep"), split_axis=0, concat_axis=0, tiled=True)
    return jnp.sum(shares, axis=0)


def solution(mesh):
    fine = Mesh(mesh.devices.reshape(8, 4, 2, 4), ("z", "y", "core", "rep"))
    pair = ("z", "y", "core")
    return jax.shard_map(
        body,
        mesh=fine,
        in_specs=(P(pair, None), P(), P(pair, "rep", None), P()),
        out_specs=P(pair, "rep"),
        check_vma=False,
    )
```

```python
import functools

import jax
import jax.numpy as jnp
from jax import lax
from jax.experimental import pallas as pl
from jax.experimental.pallas import tpu as pltpu
from jax.sharding import Mesh
from jax.sharding import PartitionSpec as P

LANES = 128
PAD = 16
VMEM = 56 * 1024 * 1024
SHIFTS = (64, 32, 16, 8, 4, 2, 1)
TOP = 8.0
FRACTION = 12


def power(exponent, sign):
    out = jnp.ones_like(exponent)
    for bit in SHIFTS:
        has = exponent >= bit
        out = jnp.where(has, out * (2.0 ** (sign * bit)), out)
        exponent = jnp.where(has, exponent - bit, exponent)
    return out


def split2(value):
    first = value.astype(jnp.bfloat16)
    return first, (value - first.astype(jnp.float32)).astype(jnp.bfloat16)


def fold_kernel(slab_ref, transform_ref, out_ref):
    rows = slab_ref[...]
    high, low = split2(transform_ref[...])
    folded = jnp.dot(rows, low, preferred_element_type=jnp.float32)
    folded = folded + jnp.dot(rows, high, preferred_element_type=jnp.float32)
    peak = jnp.max(jnp.abs(folded), axis=1, keepdims=True)
    exponent = jnp.zeros_like(peak)
    for bit in SHIFTS:
        fits = (peak * (2.0 ** bit) < TOP) & (exponent + bit <= 96)
        peak = jnp.where(fits, peak * (2.0 ** bit), peak)
        exponent = jnp.where(fits, exponent + bit, exponent)
    scaled = folded * power(exponent, 1) * (2.0 ** FRACTION)
    codes = jnp.clip(jnp.round(scaled), -32767.0, 32767.0)
    count = rows.shape[0]
    out_ref[:count] = codes.astype(jnp.int32).astype(jnp.int16)
    across = jnp.transpose(jnp.broadcast_to(exponent, (count, LANES)))
    out_ref[count:] = across[:PAD].astype(jnp.int32).astype(jnp.int16)


def fold(slabs, transform):
    rows, cols = slabs.shape[0], transform.shape[1]
    return pl.pallas_call(
        fold_kernel,
        out_shape=jax.ShapeDtypeStruct((rows + PAD, cols), jnp.int16),
        compiler_params=pltpu.CompilerParams(vmem_limit_bytes=16 << 20),
        cost_estimate=pl.CostEstimate(flops=4 * rows * slabs.shape[1] * cols, bytes_accessed=4 << 20, transcendentals=0),
        name="fold",
    )(slabs, transform)


def pick_kernel(per_device, width, sizes_ref, rep_ref, tau_hbm, out_hbm, low_ref, turn_ref, left_ref, tau_ref, stage_ref, tau_sems, out_sems):
    slabs, packed, groups = sizes_ref.shape[0], tau_ref.shape[1], stage_ref.shape[0]
    pieces, lines = tau_sems.shape[0], out_sems.shape[0]
    piece, span = packed // pieces, per_device * width

    def load(k):
        columns = pl.ds(pl.multiple_of(k * piece, piece), piece)
        return pltpu.make_async_copy(tau_hbm.at[:, columns], tau_ref.at[:, columns], tau_sems.at[k])

    for k in range(pieces):
        load(k).start()
    start = rep_ref[0] * width

    def place(s, base):
        low = jnp.minimum((base + start) & -LANES, packed - 2 * LANES)
        low_ref[s] = low
        turn_ref[s] = 2 * LANES - jnp.minimum(base + start - low, 2 * LANES - 1)
        size = sizes_ref[s]
        left_ref[s] = size - start
        return base + size

    lax.fori_loop(0, slabs, place, jnp.int32(0), unroll=16)
    lane = lax.broadcasted_iota(jnp.int32, (tau_ref.shape[0], LANES), 1)

    def arrive(k, carry):
        load(k).wait()
        return carry

    stores, have = [], jnp.int32(0)
    for z in range(lines):
        end = low_ref[(z + 1) * groups * per_device - 1] + 2 * LANES
        need = lax.div(end + piece - 1, piece) if z < lines - 1 else jnp.int32(pieces)
        lax.fori_loop(have, need, arrive, 0)
        have = need
        for group in range(groups):
            for i in range(per_device):
                slab = (z * groups + group) * per_device + i
                column = z * span + i * width
                window = tau_ref[:, pl.ds(pl.multiple_of(low_ref[slab], LANES), 2 * LANES)]
                moved = pltpu.roll(window, turn_ref[slab], axis=1)[:, :LANES]
                stage_ref[group, :, column:column + LANES] = jnp.where(lane < left_ref[slab], moved, jnp.zeros_like(moved))
        columns = pl.ds(z * span, span)
        store = pltpu.make_async_copy(stage_ref.at[:, :, columns], out_hbm.at[:, :, columns], out_sems.at[z])
        store.start()
        stores.append(store)
    for store in stores:
        store.wait()


def pick(tau, sizes, rep, groups, per_device, width):
    slabs = sizes.shape[0]
    lines = slabs // groups // per_device
    shape = (groups, tau.shape[0], lines * per_device * width)
    return pl.pallas_call(
        functools.partial(pick_kernel, per_device, width),
        in_specs=[pl.BlockSpec(memory_space=pltpu.SMEM)] * 2 + [pl.BlockSpec(memory_space=pl.ANY)],
        out_specs=pl.BlockSpec(memory_space=pl.ANY),
        out_shape=jax.ShapeDtypeStruct(shape, jnp.bfloat16),
        scratch_shapes=[pltpu.SMEM((slabs,), jnp.int32)] * 3
        + [
            pltpu.VMEM(tau.shape, jnp.bfloat16),
            pltpu.VMEM(shape, jnp.bfloat16),
            pltpu.SemaphoreType.DMA((8,)),
            pltpu.SemaphoreType.DMA((lines,)),
        ],
        compiler_params=pltpu.CompilerParams(vmem_limit_bytes=VMEM),
        cost_estimate=pl.CostEstimate(flops=0, bytes_accessed=12 << 20, transcendentals=0),
        name="pick",
    )(sizes, rep, tau)


def contract_kernel(step, core_ref, amps_hbm, coded_hbm, out_ref, amps_ref, coded_ref, amps_sems, coded_sems):
    chunks, depth = coded_ref.shape[0], coded_ref.shape[1] - PAD
    ys, reps, rows, cols = out_ref.shape
    stride = amps_hbm.shape[0] // ys
    loads = []
    for n in range(chunks // step):
        columns = pl.ds(n * step * depth, step * depth)
        load = [pltpu.make_async_copy(coded_hbm.at[pl.ds(n * step, step)], coded_ref.at[pl.ds(n * step, step)], coded_sems.at[n])]
        for y in range(ys):
            source = amps_hbm.at[y * stride + core_ref[0], :, columns]
            load.append(pltpu.make_async_copy(source, amps_ref.at[y, :, columns], amps_sems.at[n, y]))
        loads.append(load)
    for load in loads:
        for copy in load:
            copy.start()
    total = None
    for n, load in enumerate(loads):
        for copy in load:
            copy.wait()
        for k in range(n * step, (n + 1) * step):
            code = coded_ref[k, :depth].astype(jnp.int32).astype(jnp.float32)
            exponent = coded_ref[k, depth:].astype(jnp.int32).astype(jnp.float32)[:1]
            scale = power(exponent, -1) * (2.0 ** -FRACTION)
            amps = amps_ref[:, :, k * depth:(k + 1) * depth].reshape(ys * rows, depth)
            amps = amps * scale.astype(jnp.bfloat16)
            for term in split2(code):
                more = jnp.dot(amps, term, preferred_element_type=jnp.float32)
                total = more if total is None else total + more
    for y in range(ys):
        for r in range(reps):
            out_ref[y, r] = total[y * rows:(y + 1) * rows, r * cols:(r + 1) * cols]


def contract(amps, coded, core, ys, reps, grant):
    chunks, padded, cols = coded.shape
    groups, rows, depth = amps.shape
    step = 1
    shape = (ys, reps, rows, cols // reps)
    return pl.pallas_call(
        functools.partial(contract_kernel, step),
        in_specs=[pl.BlockSpec(memory_space=pltpu.SMEM)] + [pl.BlockSpec(memory_space=pl.ANY)] * 2,
        out_specs=pl.BlockSpec(memory_space=pltpu.VMEM),
        out_shape=jax.ShapeDtypeStruct(shape, jnp.float32),
        scratch_shapes=[
            pltpu.VMEM((ys, rows, depth), jnp.bfloat16),
            pltpu.VMEM(coded.shape, jnp.int16),
            pltpu.SemaphoreType.DMA((chunks // step, ys)),
            pltpu.SemaphoreType.DMA((chunks // step,)),
        ],
        compiler_params=pltpu.CompilerParams(vmem_limit_bytes=grant << 20),
        cost_estimate=pl.CostEstimate(flops=4 * ys * rows * depth * cols, bytes_accessed=7 << 20, transcendentals=0),
        name="contract",
    )(core.reshape(1), amps, coded)


def body(tau_ao, slab_sizes, integrals, transform):
    groups = lax.axis_size("y") * lax.axis_size("core")
    reps = lax.axis_size("rep")
    per_device, width, depth = integrals.shape
    coded = fold(integrals.reshape(per_device * width, depth), transform)
    line = lax.all_gather(coded, "z", axis=0, tiled=False)
    rep = lax.axis_index("rep").reshape(1)
    picked = pick(tau_ao, slab_sizes, rep, groups, per_device, width)
    arrived = lax.all_to_all(picked, ("y", "core"), split_axis=0, concat_axis=0, tiled=True)
    core, ys = lax.axis_index("core"), lax.axis_size("y")
    theirs = contract(arrived, line, 1 - core, ys, reps, 50)
    theirs = lax.ppermute(theirs, "core", [(0, 1), (1, 0)])
    partial = contract(arrived, line, core, ys, reps, 32) + theirs
    partial = partial.reshape(ys * reps, *partial.shape[2:])
    shares = lax.all_to_all(partial, ("y", "rep"), split_axis=0, concat_axis=0, tiled=True)
    return jnp.sum(shares, axis=0)


def solution(mesh):
    fine = Mesh(mesh.devices.reshape(8, 4, 2, 4), ("z", "y", "core", "rep"))
    pair = ("z", "y", "core")
    return jax.shard_map(
        body,
        mesh=fine,
        in_specs=(P(pair, None), P(), P(pair, "rep", None), P()),
        out_specs=P(pair, "rep"),
        check_vma=False,
    )
```
